32 devices in a mesh: tower: 2 (over core), section: 4 (over y, x), tp: 4 (over z).
Axes of the slice: x: 2, y: 2, z: 4, core: 2. Of those that a mesh axis runs over, the one named last changes fastest.
Arguments:
- in_flight: bfloat16 [2, 4, 430080], P('tower', 'section', 'tp'), may hold values from -6 to 6
- fresh: bfloat16 [2, 3, 430080], P('tower', None, 'tp'), may hold values from -6 to 6
- wide_proj: bfloat16 [2, 4, 2, 5120, 2048], P('tower', 'section', None, None, 'tp'), may hold values from -0.024317239 to 0.024317239
- narrow_proj: bfloat16 [2, 4, 2, 1792, 2048], P('tower', 'section', None, None, 'tp'), may hold values from -0.041103636 to 0.041103636
- gain_vis: bfloat16 [4, 1792], P('section'), may hold values from 0.25 to 1.75
- gain_txt: bfloat16 [4, 5120], P('section'), may hold values from 0.25 to 1.75
- text_len: int32 [7], replicated, may hold values from 21 to 84, as said below
- vis_len: int32 [7], replicated, may hold values from 60 to 240, as said below
Outputs:
- section_out: bfloat16 [2, 4, 4, 430080], P('tower', 'section', None, 'tp')
The draws below stay inside these ranges and needn't reach their ends.
Inputs may be any that keep to these rules, and one draw needn't show every extreme that they name: `text_len`: some micro-batch has all 84 tokens live. `vis_len`: some micro-batch has all 240 patches live.
All inputs are finite; a program needn't handle non-finite values.
Results may differ from the reference program's by a relative error of at most 0.02.
Values may be sent and summed in bfloat16 or wider, within the bound.
A program may use at most 128 MiB of HBM per device.

```python
import jax
import jax.numpy as jnp
from jax import lax

VW = 1792
TW = 5120
HEADS = 32
HDIM = 64
MB = 4
JOINT = 2048
VIS_ROWS = 240
TXT_ROWS = 84
FLAT = 107520
N_SECTION = 4
N_TP = 4


def draw_lengths(key, rows):
    count = N_SECTION + MB - 1
    lengths = jax.random.randint(key, (count,), max(1, rows // 4), rows)
    which = jax.random.randint(jax.random.fold_in(key, 7), (), 0, count)
    return lengths.at[which].set(rows).astype(jnp.int32)


def draw_text_len(key, part):
    key = jax.random.fold_in(key, 1)
    return draw_lengths(key, TXT_ROWS)


def draw_vis_len(key, part):
    key = jax.random.fold_in(key, 2)
    return draw_lengths(key, VIS_ROWS)


def draw_wide_proj(key, part):
    key = jax.random.fold_in(key, 3)
    spread = jax.random.uniform(key, (2, N_SECTION, 2, TW, JOINT), jnp.float32, -1.0, 1.0)
    return (spread * (1.73 * TW ** (-0.5))).astype(jnp.bfloat16)


def draw_narrow_proj(key, part):
    key = jax.random.fold_in(key, 4)
    spread = jax.random.uniform(key, (2, N_SECTION, 2, VW, JOINT), jnp.float32, -1.0, 1.0)
    return (spread * (1.73 * VW ** (-0.5))).astype(jnp.bfloat16)


def level_of(own_key, dims, shards, smallest, largest):
    def one(axis_at, blocks):
        steps = jax.random.uniform(jax.random.fold_in(jax.random.fold_in(own_key, 6), axis_at), (blocks,), jnp.float32, smallest / len(shards), largest / len(shards))
        return jnp.repeat(jnp.exp(steps), dims[axis_at] // blocks).reshape((-1,) + (1,) * (len(dims) - axis_at - 1))

    level = one(*shards[0])
    for cut in shards[1:]:
        level = level * one(*cut)
    return level


def bell_draw(own_key, dims, scale, bound, shards=(), held_as=jnp.bfloat16):
    array = jax.random.normal(own_key, dims, jnp.float32) * scale
    if len(shards) > 0:
        array = level_of(own_key, dims, shards, -0.22, 0.18) * array
    return jnp.clip(array, min=-bound, max=bound).astype(held_as)


def setup_inputs(seed: int = 0) -> dict:
    key_of = jax.random.split(jax.random.key(seed), 9)
    in_flight = bell_draw(key_of[0], (2, N_SECTION, N_TP * FLAT), 1.0, 6.0, ((0, 2), (1, 4), (2, 4)))
    fresh = bell_draw(key_of[1], (2, MB - 1, N_TP * FLAT), 1.0, 6.0, ((0, 2), (2, 4)))
    wide_proj = draw_wide_proj(jax.random.fold_in(key_of[8], 71), 0)
    narrow_proj = draw_narrow_proj(jax.random.fold_in(key_of[8], 71), 0)
    gain_vis = jnp.clip(1.0 + 0.15 * jax.random.normal(key_of[4], (N_SECTION, VW), jnp.float32), 0.25, 1.75).astype(jnp.bfloat16)
    gain_txt = jnp.clip(1.0 + 0.15 * jax.random.normal(key_of[5], (N_SECTION, TW), jnp.float32), 0.25, 1.75).astype(jnp.bfloat16)
    text_len = draw_text_len(jax.random.fold_in(key_of[8], 71), 0)
    vis_len = draw_vis_len(jax.random.fold_in(key_of[8], 71), 0)
    return dict(in_flight=in_flight, fresh=fresh, wide_proj=wide_proj, narrow_proj=narrow_proj, gain_vis=gain_vis, gain_txt=gain_txt, text_len=text_len, vis_len=vis_len)


def normed(stream, gain):
    values = stream.astype(jnp.float32)
    scale = lax.rsqrt(lax.optimization_barrier(jnp.mean(values * values, axis=-1, keepdims=True)) + 1e-06)
    return (values * scale * gain.astype(jnp.float32)).astype(jnp.bfloat16)

def unpack(packed, rows, width):
    return packed.reshape(N_TP, rows, width // N_TP).transpose(1, 0, 2).reshape(rows, width)

def pack(full, rows, width):
    return full.reshape(rows, N_TP, width // N_TP).transpose(1, 0, 2).reshape(-1)

def cross(query_src, key_src, query_w, key_w, value_w, out_w, live):
    rows_q = query_src.shape[0]
    rows_k = key_src.shape[0]
    query = jnp.dot(query_src, query_w, preferred_element_type=jnp.float32).astype(jnp.bfloat16)
    keys = jnp.dot(key_src, key_w, preferred_element_type=jnp.float32).astype(jnp.bfloat16)
    values = jnp.dot(key_src, value_w, preferred_element_type=jnp.float32).astype(jnp.bfloat16)
    query = query.reshape(rows_q, HEADS, HDIM).astype(jnp.float32)
    keys = keys.reshape(rows_k, HEADS, HDIM).astype(jnp.float32)
    values = values.reshape(rows_k, HEADS, HDIM).astype(jnp.float32)
    scores = jnp.einsum('qhd,khd->hqk', query, keys) / jnp.sqrt(jnp.float32(HDIM))
    alive = jnp.arange(rows_k, dtype=jnp.int32) < live
    scores = jnp.where(alive[None, None, :], scores, jnp.float32(-1e+30))
    weights = jnp.exp(scores)
    probs = (weights / lax.optimization_barrier(jnp.sum(weights, axis=-1, keepdims=True))).astype(jnp.bfloat16)
    attended = jnp.einsum('hqk,khd->qhd', probs.astype(jnp.float32), values).astype(jnp.bfloat16)
    share = JOINT // N_TP
    grouped = attended.reshape(rows_q, N_TP, share).astype(jnp.float32)
    out_groups = out_w.astype(jnp.float32).reshape(out_w.shape[0], N_TP, share)
    partial_terms = jnp.einsum('qgj,wgj->gqw', grouped, out_groups).astype(jnp.bfloat16)
    return lax.optimization_barrier(jnp.sum(partial_terms.astype(jnp.float32), axis=0))

def reference(in_flight, fresh, wide_proj, narrow_proj, gain_vis, gain_txt, text_len, vis_len):
    vision_rec = []
    text_rec = []
    previous_vis = None
    previous_txt = None
    for tick in range(MB):
        vis_now = []
        txt_now = []
        for section in range(N_SECTION):
            if tick == 0:
                vis_packed = in_flight[0, section]
                txt_packed = in_flight[1, section]
            elif section == 0:
                vis_packed = fresh[0, tick - 1]
                txt_packed = fresh[1, tick - 1]
            else:
                vis_packed = previous_vis[section - 1]
                txt_packed = previous_txt[section - 1]
            flight = tick - section + N_SECTION - 1
            vision = unpack(vis_packed, VIS_ROWS, VW)
            text = unpack(txt_packed, TXT_ROWS, TW)
            norm_vis = normed(vision, gain_vis[section])
            norm_txt = normed(text, gain_txt[section])
            delta_vis = cross(norm_vis, norm_txt, narrow_proj[0, section, 0], wide_proj[0, section, 0], wide_proj[0, section, 1], narrow_proj[0, section, 1], text_len[flight])
            delta_txt = cross(norm_txt, norm_vis, wide_proj[1, section, 0], narrow_proj[1, section, 0], narrow_proj[1, section, 1], wide_proj[1, section, 1], vis_len[flight])
            vision = (vision.astype(jnp.float32) + delta_vis).astype(jnp.bfloat16)
            text = (text.astype(jnp.float32) + delta_txt).astype(jnp.bfloat16)
            vis_now.append(pack(vision, VIS_ROWS, VW))
            txt_now.append(pack(text, TXT_ROWS, TW))
        previous_vis = vis_now
        previous_txt = txt_now
        vision_rec.append(jnp.stack(vis_now))
        text_rec.append(jnp.stack(txt_now))
    vision_all = jnp.stack(vision_rec, axis=1)
    text_all = jnp.stack(text_rec, axis=1)
    return jnp.stack([vision_all, text_all])
```

```python
import functools

import jax
import jax.numpy as jnp
from jax import lax
from jax.experimental import pallas as pl
from jax.experimental.pallas import tpu as pltpu
from jax.sharding import PartitionSpec as P

HDIM = 64
MESH = pl.DeviceIdType.MESH
F32 = jnp.float32
BF16 = jnp.bfloat16


def remote(src, dst, send_sem, recv_sem, where):
    return pltpu.make_async_remote_copy(
        src_ref=src, dst_ref=dst, send_sem=send_sem, recv_sem=recv_sem,
        device_id=where, device_id_type=MESH,
    )


def dot_nt(a, b):
    return lax.dot_general(a, b, (((1,), (1,)), ((), ())), preferred_element_type=F32)


def attend(q_ref, k_ref, v_ref, att_ref, live):
    rows_q, joint = q_ref.shape
    rows_k = k_ref.shape[0]
    alive = lax.broadcasted_iota(jnp.int32, (rows_q, rows_k), 1) < live
    lane = lax.broadcasted_iota(jnp.int32, (1, 128), 1) // HDIM
    for at in range(0, joint, 128):
        query = q_ref[:, at:at + 128]
        keys = k_ref[:, at:at + 128]
        values = v_ref[:, at:at + 128]
        total = None
        for head in range(128 // HDIM):
            mask = (lane == head).astype(F32).astype(BF16)
            scores = dot_nt(query, keys * mask) * (HDIM ** -0.5)
            weights = jnp.exp(jnp.where(alive, scores, -1e30))
            probs = (weights / jnp.sum(weights, axis=-1, keepdims=True)).astype(BF16)
            part = jnp.dot(probs, values * mask, preferred_element_type=F32)
            total = part if total is None else total + part
        att_ref[:, at:at + 128] = total.astype(BF16)


def kernel(sections, groups, ticks, txt_len, vis_len, gain_v, gain_t, in_v, in_t, wide_hbm, narrow_hbm,
           out_v, out_t,
           wide, narrow, all_v, all_t, send_v, send_t, got_v, got_t,
           acc_v, acc_ka, acc_kb, acc_t, acc_kc, acc_kd, ssq_v, ssq_t,
           q_v, k_v, v_v, q_t, k_t, v_t,
           weight_sem, load_sem, ag_send, ag_recv, fw_send, fw_recv, rs_send, rs_recv, sh_send, sh_recv):
    tower = lax.axis_index("tower")
    section = lax.axis_index("section")
    me = lax.axis_index("tp")

    weight_copies = [
        pltpu.make_async_copy(narrow_hbm, narrow, weight_sem.at[0]),
        pltpu.make_async_copy(wide_hbm, wide, weight_sem.at[1]),
    ]

    barrier = pltpu.get_barrier_semaphore()

    def greet(d, _):
        pl.semaphore_signal(barrier, inc=1, device_id={"tp": lax.rem(me + d, groups)}, device_id_type=MESH)
        return 0

    lax.fori_loop(1, groups, greet, 0)
    pl.semaphore_signal(barrier, inc=1, device_id={"tower": 1 - tower}, device_id_type=MESH)

    @pl.when(section > 0)
    def _():
        pl.semaphore_signal(barrier, inc=1, device_id={"section": section - 1}, device_id_type=MESH)

    @pl.when(section < sections - 1)
    def _():
        pl.semaphore_signal(barrier, inc=1, device_id={"section": section + 1}, device_id_type=MESH)

    def side(vision):
        mine, other = (all_v, all_t) if vision else (all_t, all_v)
        inputs = in_v if vision else in_t
        send, got, out = (send_v, got_v, out_v) if vision else (send_t, got_t, out_t)
        gain_mine, gain_other = (gain_v, gain_t) if vision else (gain_t, gain_v)
        w_mine, w_other = (narrow, wide) if vision else (wide, narrow)
        query_w = (w_mine, 0)
        key_w, value_w = (w_other, 0), (w_other, 1)
        out_w = (w_mine, 1)
        acc_q, acc_k, acc_val = (acc_v, acc_ka, acc_kb) if vision else (acc_t, acc_kc, acc_kd)
        ssq_q, ssq_k = (ssq_v, ssq_t) if vision else (ssq_t, ssq_v)
        q_ref, k_ref, v_ref = (q_v, k_v, v_v) if vision else (q_t, k_t, v_t)
        lengths = txt_len if vision else vis_len
        part = mine.shape[-1]
        part_other = other.shape[-1]
        width = part * groups
        width_other = part_other * groups
        partner = {"tower": 1 - tower}

        def load(t):
            return pltpu.make_async_copy(inputs.at[t], mine.at[t, me], load_sem.at[t])

        load(0).start()

        @pl.when(section == 0)
        def _():
            for t in range(1, ticks):
                load(t).start()

        for copy in weight_copies:
            copy.start()

        pl.semaphore_wait(
            barrier,
            groups + (section > 0).astype(jnp.int32) + (section < sections - 1).astype(jnp.int32),
        )
        load(0).wait()

        def tick_body(t, _):
            @pl.when(t > 0)
            def _():
                @pl.when(section == 0)
                def _():
                    load(t).wait()

                @pl.when(section > 0)
                def _():
                    remote(out.at[t - 1], mine.at[t, me], sh_send.at[t - 1], sh_recv.at[t], {"section": section - 1}).wait_recv()

            def ag(d):
                return remote(mine.at[t, me], mine.at[t, me], ag_send.at[d], ag_recv.at[t, d], {"tp": lax.rem(me + d, groups)})

            def ag_in(d):
                source = lax.rem(me - d + groups, groups)
                return remote(mine.at[t, source], mine.at[t, source], ag_send.at[d], ag_recv.at[t, d], {"tp": lax.rem(me + d, groups)})

            def fw(d):
                source = lax.rem(me - d + groups, groups)
                return remote(mine.at[t, source], mine.at[t, source], fw_send.at[d], fw_recv.at[t, d], partner)

            def fw_in(d):
                source = lax.rem(me - d + groups, groups)
                return remote(other.at[t, source], other.at[t, source], fw_send.at[d], fw_recv.at[t, d], partner)

            def rs(d):
                return remote(send.at[d], got.at[t, d], rs_send.at[d], rs_recv.at[t, d], {"tp": lax.rem(me + d, groups)})

            def each(body, first=0):
                def step(d, _):
                    body(d)
                    return 0
                lax.fori_loop(first, groups, step, 0)

            each(lambda d: ag(d).start(), 1)
            fw(0).start()

            @pl.when(t == 0)
            def _():
                for copy in weight_copies:
                    copy.wait()

            acc_q[...] = jnp.zeros_like(acc_q)
            acc_k[...] = jnp.zeros_like(acc_k)
            acc_val[...] = jnp.zeros_like(acc_val)
            ssq_q[...] = jnp.zeros_like(ssq_q)
            ssq_k[...] = jnp.zeros_like(ssq_k)

            def weight_rows(w, source, count):
                ref, which = w
                return ref[which, pl.ds(pl.multiple_of(source * count, 16), count), :]

            def query_block(d):
                source = lax.rem(me - d + groups, groups)
                x = mine[t, source].astype(F32)
                ssq_q[...] += jnp.sum(x * x, axis=-1, keepdims=True)
                x = (x * gain_mine[source].astype(F32)).astype(BF16)
                acc_q[...] += jnp.dot(x, weight_rows(query_w, source, part), preferred_element_type=F32)

            def key_block(d):
                source = lax.rem(me - d + groups, groups)
                fw_in(d).wait_recv()
                x = other[t, source].astype(F32)
                ssq_k[...] += jnp.sum(x * x, axis=-1, keepdims=True)
                x = (x * gain_other[source].astype(F32)).astype(BF16)
                acc_k[...] += jnp.dot(x, weight_rows(key_w, source, part_other), preferred_element_type=F32)
                acc_val[...] += jnp.dot(x, weight_rows(value_w, source, part_other), preferred_element_type=F32)

            query_block(0)
            key_block(0)

            def arrive(d):
                ag_in(d).wait_recv()
                fw(d).start()
                query_block(d)
                key_block(d)

            each(arrive, 1)

            scale_q = lax.rsqrt(ssq_q[...] * (1.0 / width) + 1e-06)
            scale_k = lax.rsqrt(ssq_k[...] * (1.0 / width_other) + 1e-06)
            q_ref[...] = (acc_q[...] * scale_q).astype(BF16)
            k_ref[...] = (acc_k[...] * scale_k).astype(BF16)
            v_ref[...] = (acc_val[...] * scale_k).astype(BF16)
            live = lengths[t - section + sections - 1]
            attend(q_ref, k_ref, v_ref, q_ref, live)

            def project(target):
                return dot_nt(q_ref[...], weight_rows(out_w, target, part)).astype(BF16)

            def emit(d):
                send[d] = project(lax.rem(me + d, groups))
                rs(d).start()

            each(emit, 1)
            send[0] = project(me)

            def collect(d):
                rs(d).wait_recv()

            each(collect, 1)
            total = mine[t, me].astype(F32) + send[0].astype(F32)
            for d in range(1, groups):
                total = total + got[t, d].astype(F32)
            out[t] = total.astype(BF16)

            @pl.when((section < sections - 1) & (t < ticks - 1))
            def _():
                remote(out.at[t], mine.at[t + 1, me], sh_send.at[t], sh_recv.at[t + 1], {"section": section + 1}).start()

            def drain(d):
                ag(d).wait_send()
                rs(d).wait_send()
                fw(d).wait_send()

            each(drain, 1)
            fw(0).wait_send()
            return 0

        lax.fori_loop(0, ticks, tick_body, 0)

        @pl.when(section < sections - 1)
        def _():
            for t in range(ticks - 1):
                remote(out.at[t], mine.at[t + 1, me], sh_send.at[t], sh_recv.at[t + 1], {"section": section + 1}).wait_send()

    pl.when(tower == 0)(lambda: side(True))
    pl.when(tower == 1)(lambda: side(False))


def on_device(in_flight, fresh, wide_proj, narrow_proj, gain_vis, gain_txt, text_len, vis_len):
    sections = lax.axis_size("section")
    groups = lax.axis_size("tp")
    flat = in_flight.shape[2]
    ticks = fresh.shape[1] + 1
    vis_width = gain_vis.shape[1]
    txt_width = gain_txt.shape[1]
    vis_rows = flat * groups // vis_width
    txt_rows = flat * groups // txt_width
    pad_v = -(-vis_rows // 16) * 16
    pad_t = -(-txt_rows // 16) * 16
    part_v = vis_width // groups
    part_t = txt_width // groups
    joint = wide_proj.shape[-1]
    first_vis = lax.axis_index("tower") == 0

    streams = jnp.concatenate([in_flight[0, :1], fresh[0]], axis=0)
    in_v = jnp.pad(streams.reshape(ticks, vis_rows, part_v), ((0, 0), (0, pad_v - vis_rows), (0, 0)))
    in_t = jnp.pad(streams.reshape(ticks, txt_rows, part_t), ((0, 0), (0, pad_t - txt_rows), (0, 0)))
    gain_v = gain_vis[0].reshape(groups, 1, part_v)
    gain_t = gain_txt[0].reshape(groups, 1, part_t)

    vmem = pl.BlockSpec(memory_space=pltpu.VMEM)
    smem = pl.BlockSpec(memory_space=pltpu.SMEM)
    anywhere = pl.BlockSpec(memory_space=pl.ANY)
    out_v, out_t = pl.pallas_call(
        functools.partial(kernel, sections, groups, ticks),
        out_shape=(
            jax.ShapeDtypeStruct((ticks, pad_v, part_v), BF16),
            jax.ShapeDtypeStruct((ticks, pad_t, part_t), BF16),
        ),
        in_specs=[smem, smem, vmem, vmem, anywhere, anywhere, anywhere, anywhere],
        out_specs=(vmem, vmem),
        scratch_shapes=[
            pltpu.VMEM(wide_proj.shape[2:], BF16),
            pltpu.VMEM(narrow_proj.shape[2:], BF16),
            pltpu.VMEM((ticks, groups, pad_v, part_v), BF16),
            pltpu.VMEM((ticks, groups, pad_t, part_t), BF16),
            pltpu.VMEM((groups, pad_v, part_v), BF16),
            pltpu.VMEM((groups, pad_t, part_t), BF16),
            pltpu.VMEM((ticks, groups, pad_v, part_v), BF16),
            pltpu.VMEM((ticks, groups, pad_t, part_t), BF16),
            pltpu.VMEM((pad_v, joint), F32),
            pltpu.VMEM((pad_t, joint), F32),
            pltpu.VMEM((pad_t, joint), F32),
            pltpu.VMEM((pad_t, joint), F32),
            pltpu.VMEM((pad_v, joint), F32),
            pltpu.VMEM((pad_v, joint), F32),
            pltpu.VMEM((pad_v, 1), F32),
            pltpu.VMEM((pad_t, 1), F32),
            pltpu.VMEM((pad_v, joint), BF16),
            pltpu.VMEM((pad_t, joint), BF16),
            pltpu.VMEM((pad_t, joint), BF16),
            pltpu.VMEM((pad_t, joint), BF16),
            pltpu.VMEM((pad_v, joint), BF16),
            pltpu.VMEM((pad_v, joint), BF16),
            pltpu.SemaphoreType.DMA((2,)),
            pltpu.SemaphoreType.DMA((ticks,)),
            pltpu.SemaphoreType.DMA((groups,)),
            pltpu.SemaphoreType.DMA((ticks, groups)),
            pltpu.SemaphoreType.DMA((groups,)),
            pltpu.SemaphoreType.DMA((ticks, groups)),
            pltpu.SemaphoreType.DMA((groups,)),
            pltpu.SemaphoreType.DMA((ticks, groups)),
            pltpu.SemaphoreType.DMA((ticks,)),
            pltpu.SemaphoreType.DMA((ticks,)),
        ],
        compiler_params=pltpu.CompilerParams(
            collective_id=0, has_side_effects=True, vmem_limit_bytes=58 * 1024 * 1024,
        ),
    )(text_len, vis_len, gain_v, gain_t, in_v, in_t, wide_proj[0, 0], narrow_proj[0, 0])

    def as_vision():
        return out_v[:, :vis_rows].reshape(ticks, flat)

    def as_text():
        return out_t[:, :txt_rows].reshape(ticks, flat)

    return lax.cond(first_vis, as_vision, as_text).reshape(1, 1, ticks, flat)


def solution(mesh):
    placed = (
        P("tower", "section", "tp"),
        P("tower", None, "tp"),
        P("tower", "section", None, None, "tp"),
        P("tower", "section", None, None, "tp"),
        P("section", None),
        P("section", None),
        P(),
        P(),
    )
    return jax.shard_map(
        on_device,
        mesh=mesh,
        in_specs=placed,
        out_specs=P("tower", "section", None, "tp"),
        check_vma=False,
    )
```

```python
import functools

import jax
import jax.numpy as jnp
from jax import lax
from jax.experimental import pallas as pl
from jax.experimental.pallas import tpu as pltpu
from jax.sharding import PartitionSpec as P

HDIM = 64
MESH = pl.DeviceIdType.MESH
F32 = jnp.float32
BF16 = jnp.bfloat16


def remote(src, dst, send_sem, recv_sem, where):
    return pltpu.make_async_remote_copy(
        src_ref=src, dst_ref=dst, send_sem=send_sem, recv_sem=recv_sem,
        device_id=where, device_id_type=MESH,
    )


def dot_nt(a, b):
    return lax.dot_general(a, b, (((1,), (1,)), ((), ())), preferred_element_type=F32)


def attend(q_ref, k_ref, v_ref, att_ref, live):
    rows_q, joint = q_ref.shape
    rows_k = k_ref.shape[0]
    alive = lax.broadcasted_iota(jnp.int32, (rows_q, rows_k), 1) < live
    lane = lax.broadcasted_iota(jnp.int32, (1, 128), 1) // HDIM
    for at in range(0, joint, 128):
        query = q_ref[:, at:at + 128]
        keys = k_ref[:, at:at + 128]
        values = v_ref[:, at:at + 128]
        total = None
        for head in range(128 // HDIM):
            mask = (lane == head).astype(F32).astype(BF16)
            scores = dot_nt(query, keys * mask) * (HDIM ** -0.5)
            weights = jnp.exp(jnp.where(alive, scores, -1e30))
            probs = (weights / jnp.sum(weights, axis=-1, keepdims=True)).astype(BF16)
            part = jnp.dot(probs, values * mask, preferred_element_type=F32)
            total = part if total is None else total + part
        att_ref[:, at:at + 128] = total.astype(BF16)


def kernel(sections, groups, ticks, chunks, txt_len, vis_len, gain_v, gain_t, in_v, in_t, wide_hbm, narrow_hbm,
           out_v, out_t,
           wide, narrow, all_v, all_t, send_v, send_t, got_v, got_t,
           acc_v, acc_ka, acc_kb, acc_t, acc_kc, acc_kd, ssq_v, ssq_t,
           q_v, k_v, v_v, q_t, k_t, v_t, sum_v, sum_t,
           weight_sem, load_sem, ag_send, ag_recv, fw_send, fw_recv, rs_send, rs_recv, sh_send, sh_recv):
    tower = lax.axis_index("tower")
    section = lax.axis_index("section")
    me = lax.axis_index("tp")

    weight_copies = [
        pltpu.make_async_copy(narrow_hbm, narrow, weight_sem.at[0]),
        pltpu.make_async_copy(wide_hbm, wide, weight_sem.at[1]),
    ]

    barrier = pltpu.get_barrier_semaphore()
    pl.semaphore_signal(barrier, inc=1, device_id={"tower": 1 - tower}, device_id_type=MESH)
    neighbours = (me > 0, me < groups - 1, section > 0, section < sections - 1)
    count = 1
    for there, where in zip(neighbours, ({"tp": me - 1}, {"tp": me + 1}, {"section": section - 1}, {"section": section + 1})):
        count = count + there.astype(jnp.int32)

        @pl.when(there)
        def _(where=where):
            pl.semaphore_signal(barrier, inc=1, device_id=where, device_id_type=MESH)

    def side(vision):
        mine, other = (all_v, all_t) if vision else (all_t, all_v)
        inputs = in_v if vision else in_t
        send, got, out = (send_v, got_v, out_v) if vision else (send_t, got_t, out_t)
        gain_mine, gain_other = (gain_v, gain_t) if vision else (gain_t, gain_v)
        w_mine, w_other = (narrow, wide) if vision else (wide, narrow)
        query_w = (w_mine, 0)
        key_w, value_w = (w_other, 0), (w_other, 1)
        out_w = (w_mine, 1)
        acc_q, acc_k, acc_val = (acc_v, acc_ka, acc_kb) if vision else (acc_t, acc_kc, acc_kd)
        ssq_q, ssq_k = (ssq_v, ssq_t) if vision else (ssq_t, ssq_v)
        q_ref, k_ref, v_ref = (q_v, k_v, v_v) if vision else (q_t, k_t, v_t)
        lengths = txt_len if vision else vis_len
        acc_out = sum_v if vision else sum_t
        part = mine.shape[-1]
        part_other = other.shape[-1]
        width = part * groups
        width_other = part_other * groups
        partner = {"tower": 1 - tower}

        def load(t):
            return pltpu.make_async_copy(inputs.at[t], mine.at[t, me], load_sem.at[t])

        load(0).start()

        @pl.when(section == 0)
        def _():
            for t in range(1, ticks):
                load(t).start()

        for copy in weight_copies:
            copy.start()

        pl.semaphore_wait(barrier, count)
        load(0).wait()

        rows = mine.shape[2] // chunks
        last = groups - 1
        position = (me, last - me)
        ahead = (me + 1, me - 1)
        behind = (me - 1, me + 1)

        def piece(c):
            return pl.ds(c * rows, rows)

        def shift(t, c, where):
            return remote(out.at[t, piece(c)], mine.at[t + 1, me, piece(c)], sh_send.at[t, c], sh_recv.at[t + 1, c], {"section": where})

        def tick_body(t, _):
            def gather(r, k, c, source, where):
                ref = mine.at[t, source, piece(c)]
                return remote(ref, ref, ag_send.at[r, k, c], ag_recv.at[t, r, k, c], {"tp": where})

            def gather_out(r, k, c):
                return gather(r, k, c, (me - k, me + k)[r], ahead[r])

            def gather_in(r, k, c):
                return gather(r, k - 1, c, (me - k, me + k)[r], behind[r])

            def cross(ref, source):
                return remote(ref.at[t, source], ref.at[t, source], fw_send.at[source], fw_recv.at[t, source], partner)

            def destination(r, k):
                return (last - k + me, k - last + me)[r]

            def reduce_out(r, k, c):
                target = destination(r, k)
                slot = target if r == 0 else jnp.where(target == me - 1, groups, target)
                return remote(send.at[target, piece(c)], got.at[t, slot, piece(c)], rs_send.at[r, k, c], rs_recv.at[t, r, k + 1, c], {"tp": ahead[r]})

            def reduce_in(r, k, c):
                target = destination(r, k)
                slot = target if r == 0 else jnp.where(target == me, groups, target)
                ref = got.at[t, slot, piece(c)]
                return slot, remote(ref, ref, rs_send.at[r, 0, c], rs_recv.at[t, r, k, c], {"tp": behind[r]})

            @pl.when((t > 0) & (section == 0))
            def _():
                load(t).wait()

            for c in range(chunks):
                @pl.when((t > 0) & (section > 0))
                def _(c=c):
                    ref = mine.at[t, me, piece(c)]
                    remote(ref, ref, sh_send.at[0, c], sh_recv.at[t, c], {"section": section - 1}).wait_recv()

                for r in range(2):
                    @pl.when(position[r] < last)
                    def _(r=r, c=c):
                        gather_out(r, 0, c).start()

            cross(mine, me).start()

            @pl.when(t == 0)
            def _():
                for copy in weight_copies:
                    copy.wait()

            acc_q[...] = jnp.zeros_like(acc_q)
            acc_k[...] = jnp.zeros_like(acc_k)
            acc_val[...] = jnp.zeros_like(acc_val)
            ssq_q[...] = jnp.zeros_like(ssq_q)
            ssq_k[...] = jnp.zeros_like(ssq_k)

            def weight_rows(w, source, count):
                ref, which = w
                return ref[which, pl.ds(pl.multiple_of(source * count, 16), count), :]

            def query_block(source):
                x = mine[t, source].astype(F32)
                ssq_q[...] += jnp.sum(x * x, axis=-1, keepdims=True)
                x = (x * gain_mine[source].astype(F32)).astype(BF16)
                acc_q[...] += jnp.dot(x, weight_rows(query_w, source, part), preferred_element_type=F32)

            def key_block(source):
                cross(other, source).wait_recv()
                x = other[t, source].astype(F32)
                ssq_k[...] += jnp.sum(x * x, axis=-1, keepdims=True)
                x = (x * gain_other[source].astype(F32)).astype(BF16)
                acc_k[...] += jnp.dot(x, weight_rows(key_w, source, part_other), preferred_element_type=F32)
                acc_val[...] += jnp.dot(x, weight_rows(value_w, source, part_other), preferred_element_type=F32)

            query_block(me)
            key_block(me)

            def hop(k, _):
                for c in range(chunks):
                    for r in range(2):
                        @pl.when(position[r] >= k)
                        def _(r=r, c=c):
                            gather_in(r, k, c).wait_recv()

                            @pl.when(position[r] < last)
                            def _():
                                gather_out(r, k, c).start()

                for r in range(2):
                    @pl.when(position[r] >= k)
                    def _(r=r):
                        cross(mine, (me - k, me + k)[r]).start()

                def visit(r, _):
                    source = jnp.where(r == 0, me - k, me + k)

                    @pl.when((source >= 0) & (source < groups))
                    def _():
                        query_block(source)
                        key_block(source)

                    return 0

                lax.fori_loop(0, 2, visit, 0)
                return 0

            lax.fori_loop(1, groups, hop, 0)

            scale_q = lax.rsqrt(ssq_q[...] * (1.0 / width) + 1e-06)
            scale_k = lax.rsqrt(ssq_k[...] * (1.0 / width_other) + 1e-06)
            q_ref[...] = (acc_q[...] * scale_q).astype(BF16)
            k_ref[...] = (acc_k[...] * scale_k).astype(BF16)
            v_ref[...] = (acc_val[...] * scale_k).astype(BF16)
            live = lengths[t - section + sections - 1]
            attend(q_ref, k_ref, v_ref, q_ref, live)

            def project(target):
                send[target] = dot_nt(q_ref[...], weight_rows(out_w, target, part)).astype(BF16)

            def reduce_hop(k, _):
                def term(r, _):
                    @pl.when(jnp.where(r == 0, me, last - me) <= k)
                    def _():
                        project(jnp.where(r == 0, last - k + me, k - last + me))

                    return 0

                lax.fori_loop(0, 2, term, 0)
                for c in range(chunks):
                    for r in range(2):
                        @pl.when(position[r] <= k)
                        def _(r=r, c=c):
                            @pl.when(position[r] > 0)
                            def _():
                                slot, copy = reduce_in(r, k, c)
                                copy.wait_recv()
                                target = destination(r, k)
                                total = send[target, piece(c)].astype(F32) + got[t, slot, piece(c)].astype(F32)
                                send[target, piece(c)] = total.astype(BF16)

                            reduce_out(r, k, c).start()

                return 0

            lax.fori_loop(0, last, reduce_hop, 0)
            project(me)
            for c in range(chunks):
                acc_out[piece(c)] = mine[t, me, piece(c)].astype(F32) + send[me, piece(c)].astype(F32)
                for r in range(2):
                    @pl.when(position[r] > 0)
                    def _(r=r, c=c):
                        slot, copy = reduce_in(r, last, c)
                        copy.wait_recv()
                        acc_out[piece(c)] += got[t, slot, piece(c)].astype(F32)

                out[t, piece(c)] = acc_out[piece(c)].astype(BF16)

                @pl.when((section < sections - 1) & (t < ticks - 1))
                def _(c=c):
                    shift(t, c, section + 1).start()

            def drain(k, _):
                for c in range(chunks):
                    for r in range(2):
                        @pl.when((position[r] >= k) & (position[r] < last))
                        def _(r=r, c=c):
                            gather_out(r, k, c).wait_send()

                        @pl.when(position[r] <= k)
                        def _(r=r, c=c):
                            reduce_out(r, k, c).wait_send()

                cross(mine, k).wait_send()
                return 0

            lax.fori_loop(0, last, drain, 0)
            cross(mine, last).wait_send()
            return 0

        lax.fori_loop(0, ticks, tick_body, 0)

        @pl.when(section < sections - 1)
        def _():
            for t in range(ticks - 1):
                for c in range(chunks):
                    shift(t, c, section + 1).wait_send()

    pl.when(tower == 0)(lambda: side(True))
    pl.when(tower == 1)(lambda: side(False))


def on_device(in_flight, fresh, wide_proj, narrow_proj, gain_vis, gain_txt, text_len, vis_len):
    sections = lax.axis_size("section")
    groups = lax.axis_size("tp")
    flat = in_flight.shape[2]
    ticks = fresh.shape[1] + 1
    vis_width = gain_vis.shape[1]
    txt_width = gain_txt.shape[1]
    vis_rows = flat * groups // vis_width
    txt_rows = flat * groups // txt_width
    pad_v = -(-vis_rows // 16) * 16
    pad_t = -(-txt_rows // 16) * 16
    part_v = vis_width // groups
    part_t = txt_width // groups
    joint = wide_proj.shape[-1]
    chunks = 3 if groups <= 8 and pad_v % 48 == 0 and pad_t % 48 == 0 else 1
    first_vis = lax.axis_index("tower") == 0

    streams = jnp.concatenate([in_flight[0, :1], fresh[0]], axis=0)
    in_v = jnp.pad(streams.reshape(ticks, vis_rows, part_v), ((0, 0), (0, pad_v - vis_rows), (0, 0)))
    in_t = jnp.pad(streams.reshape(ticks, txt_rows, part_t), ((0, 0), (0, pad_t - txt_rows), (0, 0)))
    gain_v = gain_vis[0].reshape(groups, 1, part_v)
    gain_t = gain_txt[0].reshape(groups, 1, part_t)

    vmem = pl.BlockSpec(memory_space=pltpu.VMEM)
    smem = pl.BlockSpec(memory_space=pltpu.SMEM)
    anywhere = pl.BlockSpec(memory_space=pl.ANY)
    out_v, out_t = pl.pallas_call(
        functools.partial(kernel, sections, groups, ticks, chunks),
        out_shape=(
            jax.ShapeDtypeStruct((ticks, pad_v, part_v), BF16),
            jax.ShapeDtypeStruct((ticks, pad_t, part_t), BF16),
        ),
        in_specs=[smem, smem, vmem, vmem, anywhere, anywhere, anywhere, anywhere],
        out_specs=(vmem, vmem),
        scratch_shapes=[
            pltpu.VMEM(wide_proj.shape[2:], BF16),
            pltpu.VMEM(narrow_proj.shape[2:], BF16),
            pltpu.VMEM((ticks, groups, pad_v, part_v), BF16),
            pltpu.VMEM((ticks, groups, pad_t, part_t), BF16),
            pltpu.VMEM((groups, pad_v, part_v), BF16),
            pltpu.VMEM((groups, pad_t, part_t), BF16),
            pltpu.VMEM((ticks, groups + 1, pad_v, part_v), BF16),
            pltpu.VMEM((ticks, groups + 1, pad_t, part_t), BF16),
            pltpu.VMEM((pad_v, joint), F32),
            pltpu.VMEM((pad_t, joint), F32),
            pltpu.VMEM((pad_t, joint), F32),
            pltpu.VMEM((pad_t, joint), F32),
            pltpu.VMEM((pad_v, joint), F32),
            pltpu.VMEM((pad_v, joint), F32),
            pltpu.VMEM((pad_v, 1), F32),
            pltpu.VMEM((pad_t, 1), F32),
            pltpu.VMEM((pad_v, joint), BF16),
            pltpu.VMEM((pad_t, joint), BF16),
            pltpu.VMEM((pad_t, joint), BF16),
            pltpu.VMEM((pad_t, joint), BF16),
            pltpu.VMEM((pad_v, joint), BF16),
            pltpu.VMEM((pad_v, joint), BF16),
            pltpu.VMEM((pad_v, part_v), F32),
            pltpu.VMEM((pad_t, part_t), F32),
            pltpu.SemaphoreType.DMA((2,)),
            pltpu.SemaphoreType.DMA((ticks,)),
            pltpu.SemaphoreType.DMA((2, groups, chunks)),
            pltpu.SemaphoreType.DMA((ticks, 2, groups, chunks)),
            pltpu.SemaphoreType.DMA((groups,)),
            pltpu.SemaphoreType.DMA((ticks, groups)),
            pltpu.SemaphoreType.DMA((2, groups, chunks)),
            pltpu.SemaphoreType.DMA((ticks, 2, groups, chunks)),
            pltpu.SemaphoreType.DMA((ticks, chunks)),
            pltpu.SemaphoreType.DMA((ticks, chunks)),
        ],
        compiler_params=pltpu.CompilerParams(
            collective_id=0, has_side_effects=True, vmem_limit_bytes=58 * 1024 * 1024,
        ),
    )(text_len, vis_len, gain_v, gain_t, in_v, in_t, wide_proj[0, 0], narrow_proj[0, 0])

    def as_vision():
        return out_v[:, :vis_rows].reshape(ticks, flat)

    def as_text():
        return out_t[:, :txt_rows].reshape(ticks, flat)

    return lax.cond(first_vis, as_vision, as_text).reshape(1, 1, ticks, flat)


def solution(mesh):
    placed = (
        P("tower", "section", "tp"),
        P("tower", None, "tp"),
        P("tower", "section", None, None, "tp"),
        P("tower", "section", None, None, "tp"),
        P("section", None),
        P("section", None),
        P(),
        P(),
    )
    return jax.shard_map(
        on_device,
        mesh=mesh,
        in_specs=placed,
        out_specs=P("tower", "section", None, "tp"),
        check_vma=False,
    )
```

```python
import functools

import jax
import jax.numpy as jnp
from jax import lax
from jax.experimental import pallas as pl
from jax.experimental.pallas import tpu as pltpu
from jax.sharding import PartitionSpec as P

HDIM = 64
MESH = pl.DeviceIdType.MESH
F32 = jnp.float32
BF16 = jnp.bfloat16


def remote(src, dst, send_sem, recv_sem, where):
    return pltpu.make_async_remote_copy(
        src_ref=src, dst_ref=dst, send_sem=send_sem, recv_sem=recv_sem,
        device_id=where, device_id_type=MESH,
    )


def dot_nt(a, b):
    return lax.dot_general(a, b, (((1,), (1,)), ((), ())), preferred_element_type=F32)


def attend(q_ref, k_ref, v_ref, att_ref, live):
    rows_q, joint = q_ref.shape
    rows_k = k_ref.shape[0]
    alive = lax.broadcasted_iota(jnp.int32, (rows_q, rows_k), 1) < live
    lane = lax.broadcasted_iota(jnp.int32, (1, 128), 1) // HDIM
    for at in range(0, joint, 128):
        query = q_ref[:, at:at + 128]
        keys = k_ref[:, at:at + 128]
        values = v_ref[:, at:at + 128]
        total = None
        for head in range(128 // HDIM):
            mask = (lane == head).astype(F32).astype(BF16)
            scores = dot_nt(query, keys * mask) * (HDIM ** -0.5)
            weights = jnp.exp(jnp.where(alive, scores, -1e30))
            probs = (weights / jnp.sum(weights, axis=-1, keepdims=True)).astype(BF16)
            part = jnp.dot(probs, values * mask, preferred_element_type=F32)
            total = part if total is None else total + part
        att_ref[:, at:at + 128] = total.astype(BF16)


def kernel(sections, groups, ticks, chunks, txt_len, vis_len, gain_v, gain_t, in_v, in_t, wide_hbm, narrow_hbm,
           out_v, out_t,
           wide, narrow, all_v, all_t, send_v, send_t, got_v, got_t,
           acc_v, acc_ka, acc_kb, acc_t, acc_kc, acc_kd, ssq_v, ssq_t,
           q_v, k_v, v_v, q_t, k_t, v_t, sum_v, sum_t,
           weight_sem, load_sem, ag_send, ag_recv, fw_send, fw_recv, rs_send, rs_recv, sh_send, sh_recv):
    tower = lax.axis_index("tower")
    section = lax.axis_index("section")
    me = lax.axis_index("tp")

    weight_copies = [
        pltpu.make_async_copy(narrow_hbm, narrow, weight_sem.at[0]),
        pltpu.make_async_copy(wide_hbm, wide, weight_sem.at[1]),
    ]

    barrier = pltpu.get_barrier_semaphore()
    pl.semaphore_signal(barrier, inc=1, device_id={"tower": 1 - tower}, device_id_type=MESH)
    neighbours = (me > 0, me < groups - 1, section > 0, section < sections - 1)
    count = 1
    for there, where in zip(neighbours, ({"tp": me - 1}, {"tp": me + 1}, {"section": section - 1}, {"section": section + 1})):
        count = count + there.astype(jnp.int32)

        @pl.when(there)
        def _(where=where):
            pl.semaphore_signal(barrier, inc=1, device_id=where, device_id_type=MESH)

    def side(vision):
        mine, other = (all_v, all_t) if vision else (all_t, all_v)
        inputs = in_v if vision else in_t
        send, got, out = (send_v, got_v, out_v) if vision else (send_t, got_t, out_t)
        gain_mine, gain_other = (gain_v, gain_t) if vision else (gain_t, gain_v)
        w_mine, w_other = (narrow, wide) if vision else (wide, narrow)
        query_w = (w_mine, 0)
        key_w, value_w = (w_other, 0), (w_other, 1)
        out_w = (w_mine, 1)
        acc_q, acc_k, acc_val = (acc_v, acc_ka, acc_kb) if vision else (acc_t, acc_kc, acc_kd)
        ssq_q, ssq_k = (ssq_v, ssq_t) if vision else (ssq_t, ssq_v)
        q_ref, k_ref, v_ref = (q_v, k_v, v_v) if vision else (q_t, k_t, v_t)
        lengths = txt_len if vision else vis_len
        acc_out = sum_v if vision else sum_t
        part = mine.shape[-1]
        part_other = other.shape[-1]
        width = part * groups
        width_other = part_other * groups
        partner = {"tower": 1 - tower}

        def load(t):
            return pltpu.make_async_copy(inputs.at[t], mine.at[t, me], load_sem.at[t])

        load(0).start()

        @pl.when(section == 0)
        def _():
            for t in range(1, ticks):
                load(t).start()

        for copy in weight_copies:
            copy.start()

        pl.semaphore_wait(barrier, count)
        load(0).wait()

        rows = mine.shape[2] // chunks
        last = groups - 1
        position = (me, last - me)
        ahead = (me + 1, me - 1)
        behind = (me - 1, me + 1)

        def piece(c):
            return pl.ds(c * rows, rows)

        def shift(t, c, where):
            return remote(out.at[t, piece(c)], mine.at[t + 1, me, piece(c)], sh_send.at[t, c], sh_recv.at[t + 1, c], {"section": where})

        def tick_body(t, _):
            def gather(r, k, c, source, where):
                ref = mine.at[t, source, piece(c)]
                return remote(ref, ref, ag_send.at[r, k, c], ag_recv.at[t, r, k, c], {"tp": where})

            def gather_out(r, k, c):
                return gather(r, k, c, (me - k, me + k)[r], ahead[r])

            def gather_in(r, k, c):
                return gather(r, k - 1, c, (me - k, me + k)[r], behind[r])

            def cross(ref, source):
                return remote(ref.at[t, source], ref.at[t, source], fw_send.at[source], fw_recv.at[t, source], partner)

            def destination(r, k):
                return (last - k + me, k - last + me)[r]

            def reduce_out(r, k, c):
                target = destination(r, k)
                slot = target if r == 0 else jnp.where(target == me - 1, groups, target)
                return remote(send.at[target, piece(c)], got.at[t, slot, piece(c)], rs_send.at[r, k, c], rs_recv.at[t, r, k + 1, c], {"tp": ahead[r]})

            def reduce_in(r, k, c):
                target = destination(r, k)
                slot = target if r == 0 else jnp.where(target == me, groups, target)
                ref = got.at[t, slot, piece(c)]
                return slot, remote(ref, ref, rs_send.at[r, 0, c], rs_recv.at[t, r, k, c], {"tp": behind[r]})

            @pl.when((t > 0) & (section == 0))
            def _():
                load(t).wait()

            for c in range(chunks):
                @pl.when((t > 0) & (section > 0))
                def _(c=c):
                    ref = mine.at[t, me, piece(c)]
                    remote(ref, ref, sh_send.at[0, c], sh_recv.at[t, c], {"section": section - 1}).wait_recv()

                for r in range(2):
                    @pl.when(position[r] < last)
                    def _(r=r, c=c):
                        gather_out(r, 0, c).start()

            cross(mine, me).start()

            @pl.when(t == 0)
            def _():
                for copy in weight_copies:
                    copy.wait()

            acc_q[...] = jnp.zeros_like(acc_q)
            acc_k[...] = jnp.zeros_like(acc_k)
            acc_val[...] = jnp.zeros_like(acc_val)
            ssq_q[...] = jnp.zeros_like(ssq_q)
            ssq_k[...] = jnp.zeros_like(ssq_k)

            def weight_rows(w, source, count):
                ref, which = w
                return ref[which, pl.ds(pl.multiple_of(source * count, 16), count), :]

            def query_block(source):
                x = mine[t, source].astype(F32)
                ssq_q[...] += jnp.sum(x * x, axis=-1, keepdims=True)
                x = (x * gain_mine[source].astype(F32)).astype(BF16)
                acc_q[...] += jnp.dot(x, weight_rows(query_w, source, part), preferred_element_type=F32)

            def key_block(source):
                cross(other, source).wait_recv()
                x = other[t, source].astype(F32)
                ssq_k[...] += jnp.sum(x * x, axis=-1, keepdims=True)
                x = (x * gain_other[source].astype(F32)).astype(BF16)
                acc_k[...] += jnp.dot(x, weight_rows(key_w, source, part_other), preferred_element_type=F32)
                acc_val[...] += jnp.dot(x, weight_rows(value_w, source, part_other), preferred_element_type=F32)

            query_block(me)
            key_block(me)

            def hop(k, _):
                for c in range(chunks):
                    for r in range(2):
                        @pl.when(position[r] >= k)
                        def _(r=r, c=c):
                            gather_in(r, k, c).wait_recv()

                            @pl.when(position[r] < last)
                            def _():
                                gather_out(r, k, c).start()

                for r in range(2):
                    @pl.when(position[r] >= k)
                    def _(r=r):
                        cross(mine, (me - k, me + k)[r]).start()

                def visit(r, _):
                    source = jnp.where(r == 0, me - k, me + k)

                    @pl.when((source >= 0) & (source < groups))
                    def _():
                        query_block(source)
                        key_block(source)

                    return 0

                lax.fori_loop(0, 2, visit, 0)
                return 0

            lax.fori_loop(1, groups, hop, 0)

            scale_q = lax.rsqrt(ssq_q[...] * (1.0 / width) + 1e-06)
            scale_k = lax.rsqrt(ssq_k[...] * (1.0 / width_other) + 1e-06)
            q_ref[...] = (acc_q[...] * scale_q).astype(BF16)
            k_ref[...] = (acc_k[...] * scale_k).astype(BF16)
            v_ref[...] = (acc_val[...] * scale_k).astype(BF16)
            live = lengths[t - section + sections - 1]
            attend(q_ref, k_ref, v_ref, q_ref, live)

            def project(target):
                send[target] = dot_nt(q_ref[...], weight_rows(out_w, target, part)).astype(BF16)

            def reduce_hop(k, _):
                def term(r, _):
                    @pl.when(jnp.where(r == 0, me, last - me) <= k)
                    def _():
                        project(jnp.where(r == 0, last - k + me, k - last + me))

                    return 0

                lax.fori_loop(0, 2, term, 0)
                for c in range(chunks):
                    for r in range(2):
                        @pl.when(position[r] <= k)
                        def _(r=r, c=c):
                            @pl.when(position[r] > 0)
                            def _():
                                slot, copy = reduce_in(r, k, c)
                                copy.wait_recv()
                                target = destination(r, k)
                                total = send[target, piece(c)].astype(F32) + got[t, slot, piece(c)].astype(F32)
                                send[target, piece(c)] = total.astype(BF16)

                            reduce_out(r, k, c).start()

                return 0

            lax.fori_loop(0, last, reduce_hop, 0)
            project(me)
            for c in range(chunks):
                acc_out[piece(c)] = mine[t, me, piece(c)].astype(F32) + send[me, piece(c)].astype(F32)
                for r in range(2):
                    @pl.when(position[r] > 0)
                    def _(r=r, c=c):
                        slot, copy = reduce_in(r, last, c)
                        copy.wait_recv()
                        acc_out[piece(c)] += got[t, slot, piece(c)].astype(F32)

                out[t, piece(c)] = acc_out[piece(c)].astype(BF16)

                @pl.when((section < sections - 1) & (t < ticks - 1))
                def _(c=c):
                    shift(t, c, section + 1).start()

            def drain(k, _):
                for c in range(chunks):
                    for r in range(2):
                        @pl.when((position[r] >= k) & (position[r] < last))
                        def _(r=r, c=c):
                            gather_out(r, k, c).wait_send()

                        @pl.when(position[r] <= k)
                        def _(r=r, c=c):
                            reduce_out(r, k, c).wait_send()

                cross(mine, k).wait_send()
                return 0

            lax.fori_loop(0, last, drain, 0)
            cross(mine, last).wait_send()
            return 0

        lax.fori_loop(0, ticks, tick_body, 0)

        @pl.when(section < sections - 1)
        def _():
            for t in range(ticks - 1):
                for c in range(chunks):
                    shift(t, c, section + 1).wait_send()

    pl.when(tower == 0)(lambda: side(True))
    pl.when(tower == 1)(lambda: side(False))


def on_device(in_flight, fresh, wide_proj, narrow_proj, gain_vis, gain_txt, text_len, vis_len):
    sections = lax.axis_size("section")
    groups = lax.axis_size("tp")
    flat = in_flight.shape[2]
    ticks = fresh.shape[1] + 1
    vis_width = gain_vis.shape[1]
    txt_width = gain_txt.shape[1]
    vis_rows = flat * groups // vis_width
    txt_rows = flat * groups // txt_width
    pad_v = -(-vis_rows // 16) * 16
    pad_t = -(-txt_rows // 16) * 16
    part_v = vis_width // groups
    part_t = txt_width // groups
    joint = wide_proj.shape[-1]
    chunks = 3 if groups <= 8 and pad_v % 48 == 0 and pad_t % 48 == 0 else 1
    first_vis = lax.axis_index("tower") == 0

    streams = jnp.concatenate([in_flight[0, :1], fresh[0]], axis=0)
    def shaped(rows, padded, part):
        return jnp.pad(streams.reshape(ticks, rows, part), ((0, 0), (0, padded - rows), (0, 0)))

    in_v, in_t = lax.cond(
        first_vis,
        lambda: (shaped(vis_rows, pad_v, part_v), jnp.zeros((ticks, pad_t, part_t), BF16)),
        lambda: (jnp.zeros((ticks, pad_v, part_v), BF16), shaped(txt_rows, pad_t, part_t)),
    )
    gain_v = gain_vis[0].reshape(groups, 1, part_v)
    gain_t = gain_txt[0].reshape(groups, 1, part_t)

    vmem = pl.BlockSpec(memory_space=pltpu.VMEM)
    smem = pl.BlockSpec(memory_space=pltpu.SMEM)
    anywhere = pl.BlockSpec(memory_space=pl.ANY)
    out_v, out_t = pl.pallas_call(
        functools.partial(kernel, sections, groups, ticks, chunks),
        out_shape=(
            jax.ShapeDtypeStruct((ticks, pad_v, part_v), BF16),
            jax.ShapeDtypeStruct((ticks, pad_t, part_t), BF16),
        ),
        in_specs=[smem, smem, vmem, vmem, anywhere, anywhere, anywhere, anywhere],
        out_specs=(vmem, vmem),
        scratch_shapes=[
            pltpu.VMEM(wide_proj.shape[2:], BF16),
            pltpu.VMEM(narrow_proj.shape[2:], BF16),
            pltpu.VMEM((ticks, groups, pad_v, part_v), BF16),
            pltpu.VMEM((ticks, groups, pad_t, part_t), BF16),
            pltpu.VMEM((groups, pad_v, part_v), BF16),
            pltpu.VMEM((groups, pad_t, part_t), BF16),
            pltpu.VMEM((ticks, groups + 1, pad_v, part_v), BF16),
            pltpu.VMEM((ticks, groups + 1, pad_t, part_t), BF16),
            pltpu.VMEM((pad_v, joint), F32),
            pltpu.VMEM((pad_t, joint), F32),
            pltpu.VMEM((pad_t, joint), F32),
            pltpu.VMEM((pad_t, joint), F32),
            pltpu.VMEM((pad_v, joint), F32),
            pltpu.VMEM((pad_v, joint), F32),
            pltpu.VMEM((pad_v, 1), F32),
            pltpu.VMEM((pad_t, 1), F32),
            pltpu.VMEM((pad_v, joint), BF16),
            pltpu.VMEM((pad_t, joint), BF16),
            pltpu.VMEM((pad_t, joint), BF16),
            pltpu.VMEM((pad_t, joint), BF16),
            pltpu.VMEM((pad_v, joint), BF16),
            pltpu.VMEM((pad_v, joint), BF16),
            pltpu.VMEM((pad_v, part_v), F32),
            pltpu.VMEM((pad_t, part_t), F32),
            pltpu.SemaphoreType.DMA((2,)),
            pltpu.SemaphoreType.DMA((ticks,)),
            pltpu.SemaphoreType.DMA((2, groups, chunks)),
            pltpu.SemaphoreType.DMA((ticks, 2, groups, chunks)),
            pltpu.SemaphoreType.DMA((groups,)),
            pltpu.SemaphoreType.DMA((ticks, groups)),
            pltpu.SemaphoreType.DMA((2, groups, chunks)),
            pltpu.SemaphoreType.DMA((ticks, 2, groups, chunks)),
            pltpu.SemaphoreType.DMA((ticks, chunks)),
            pltpu.SemaphoreType.DMA((ticks, chunks)),
        ],
        compiler_params=pltpu.CompilerParams(
            collective_id=0, has_side_effects=True, vmem_limit_bytes=58 * 1024 * 1024,
        ),
    )(text_len, vis_len, gain_v, gain_t, in_v, in_t, wide_proj[0, 0], narrow_proj[0, 0])

    def as_vision():
        return out_v[:, :vis_rows].reshape(ticks, flat)

    def as_text():
        return out_t[:, :txt_rows].reshape(ticks, flat)

    return lax.cond(first_vis, as_vision, as_text).reshape(1, 1, ticks, flat)


def solution(mesh):
    placed = (
        P("tower", "section", "tp"),
        P("tower", None, "tp"),
        P("tower", "section", None, None, "tp"),
        P("tower", "section", None, None, "tp"),
        P("section", None),
        P("section", None),
        P(),
        P(),
    )
    return jax.shard_map(
        on_device,
        mesh=mesh,
        in_specs=placed,
        out_specs=P("tower", "section", None, "tp"),
        check_vma=False,
    )
```
